256 devices in a mesh: dp: 4 (over y), expert: 64 (over x, z, core).
Axes of the slice: x: 4, y: 4, z: 8, core: 2. Of those that a mesh axis runs over, the one named last changes fastest.
Arguments:
- tokens: bfloat16 [8192, 2048], P(('dp', 'expert')), may hold values from -6 to 6
- expert_ids: int32 [8192, 8], P(('dp', 'expert')), may hold values from 0 to 63, all different within a row; in each aligned block of 32 rows (0 to 31, 32 to 63, ...) at most 8 rows name the same one
- gate_probs: float32 [8192, 8], P(('dp', 'expert')), may hold values from 0.1 to 1
- grad_out: bfloat16 [8192, 2048], P(('dp', 'expert')), may hold values from -1.1953125 to 1.1953125
- w_gate: bfloat16 [64, 2048, 768], P('expert', 'dp'), may hold values from -0.125 to 0.125
- w_up: bfloat16 [64, 2048, 768], P('expert', 'dp'), may hold values from -0.125 to 0.125
- w_down: bfloat16 [64, 768, 2048], P('expert', None, 'dp'), may hold values from -0.21875 to 0.21875
Outputs:
- layer_out: bfloat16 [8192, 2048], P(('dp', 'expert'))
- grad_tokens: bfloat16 [8192, 2048], P(('dp', 'expert'))
- grad_probs: float32 [8192, 8], P(('dp', 'expert'))
- grad_gate: bfloat16 [64, 2048, 768], P('expert', 'dp')
- grad_up: bfloat16 [64, 2048, 768], P('expert', 'dp')
- grad_down: bfloat16 [64, 768, 2048], P('expert', None, 'dp')
The draws below stay inside these ranges and needn't reach their ends.
Inputs may be any that keep to these rules, and one draw needn't show every extreme that they name: `expert_ids`: each row names 8 different experts. Within the 32 rows of one device no expert is named by more than 8 rows, a bound that some of them reach.
All inputs are finite; a program needn't handle non-finite values.
Results may differ from the reference program's by a relative error of at most 0.0064.
Values may be sent and summed in bfloat16 or wider, within the bound.
No kernel may reach another device: no remote copies, remote signals or barrier semaphores. Data moves between devices by JAX's collectives and lax.ppermute only.
A program may use at most 128 MiB of HBM per device.

```python
import math
import jax
import jax.numpy as jnp
import numpy as np
from jax import lax

D = 2048
FF = 768
TOP = 8
TOK_DEV = 32
EXPERTS = 64
MOST = 8
TOKENS = 8192
N_DP = 4
N_EXPERT = 64


def steps_of(rng, shape, shards, low, high):
    def one(dim, shards_of):
        draws = jax.random.uniform(jax.random.fold_in(jax.random.fold_in(rng, 6), dim), (shards_of,), jnp.float32, low / len(shards), high / len(shards))
        return jnp.repeat(jnp.exp(draws), shape[dim] // shards_of).reshape((-1,) + (1,) * (len(shape) - dim - 1))

    level = one(*shards[0])
    for cut in shards[1:]:
        level = level * one(*cut)
    return level


def assign_block(key, own, number, rows, number_of, top, most, lean):
    ranking = jax.random.permutation(key, number_of)
    crowded, ordinary = shares(number_of, rows * top, most, lean, True), shares(number_of, rows * top, most, lean, False)
    places = jnp.arange(number_of)

    def named(tallies, offset_by):
        used = int((tallies > 0).sum())
        fixed = max(1, used // 4)
        moved = fixed + (places - fixed + offset_by * (used - fixed)) % max(1, number_of - fixed)
        return jnp.zeros((number_of,), jnp.int32).at[ranking[jnp.where(places < fixed, places, moved)]].set(jnp.asarray(tallies, jnp.int32))

    tallies = jnp.where(number % 4 == 0, named(crowded, number // 4), named(ordinary, number - number // 4 - 1))
    mixed = jax.random.permutation(jax.random.fold_in(own, 3), number_of)
    giver, taker = mixed[0:number_of // 2 * 2:2], mixed[1:number_of // 2 * 2:2]
    margin = jnp.minimum(tallies[giver] - 1, most - tallies[taker]) // 2
    margin = jnp.where((giver == ranking[0]) | (taker == ranking[0]) | (tallies[taker] == 0), 0, jnp.maximum(margin, 0))
    moved = jax.random.randint(jax.random.fold_in(own, 4), (number_of // 2,), 0, 1 << 20) % (margin + 1)
    tallies = tallies.at[giver].add(-moved).at[taker].add(moved)
    items = jnp.searchsorted(jnp.cumsum(tallies), jnp.arange(rows * top), side="right").astype(jnp.int32)
    grid = items.reshape(top, rows).T
    grid = grid[jax.random.permutation(jax.random.fold_in(own, 1), rows)]
    offset_by = jax.random.randint(jax.random.fold_in(own, 2), (rows, 1), 0, top)
    return jnp.take_along_axis(grid, (jnp.arange(top)[None, :] + offset_by) % top, axis=1)


def shares(count, total, limit, slope, full):
    weights = [(1 << 20) // math.isqrt(grade ** slope) + 1 for grade in range(1, count + 1)]
    largest = limit if full else min(limit, max(-(-total // count), total * weights[0] // sum(weights)))
    least = 1 if total - largest >= count - 1 else 0
    holding, spare = [largest] + [least] * (count - 1), total - largest - least * (count - 1)
    while spare > 0:
        candidates = [i for i in range(1, count) if holding[i] < largest] or [i for i in range(1, count) if holding[i] < limit]
        whole, left = sum([weights[i] for i in candidates]), spare
        for i in candidates:
            addition = min(limit - holding[i], max(1, left * weights[i] // whole), spare)
            holding[i] = holding[i] + addition
            spare = spare - addition
    return np.array(holding)


def bell_draw(own_key, dims, spread, reach, split=(), held_as=jnp.bfloat16):
    result = spread * jax.random.normal(own_key, dims, jnp.float32)
    if split:
        result = result * steps_of(own_key, dims, split, -0.22, 0.18)
    return jnp.clip(result, -reach, reach).astype(held_as)


def setup_inputs(seed: int = 0) -> dict:
    streams_of = jax.random.split(jax.random.key(seed), 8)
    tokens = bell_draw(streams_of[0], (TOKENS, D), 1.0, 6.0, ((0, 256),))
    expert_ids_keys = jax.random.split(jax.random.fold_in(streams_of[1], 1), TOKENS // TOK_DEV)
    expert_ids_turns = jax.random.permutation(jax.random.fold_in(streams_of[1], 3), TOKENS // TOK_DEV)
    expert_ids = jax.vmap(lambda own, number: assign_block(jax.random.fold_in(streams_of[1], 2), own, number, TOK_DEV, EXPERTS, TOP, MOST, 2))(expert_ids_keys, expert_ids_turns).reshape((TOKENS, TOP))
    gate_probs = jnp.clip(jnp.exp(math.log(1.0) - 2.3025851 * jax.random.uniform(streams_of[2], (TOKENS, TOP), jnp.float32) ** steps_of(streams_of[2], (TOKENS, TOP), ((0, 256),), -0.2, 0.2)), 0.1, 1.0)
    grad_out = bell_draw(streams_of[3], (TOKENS, D), 0.2, 1.1953125, ((0, 256),))
    w_gate = bell_draw(streams_of[4], (EXPERTS, D, FF), D ** -0.5, 0.125, ((0, 64), (1, 4)))
    w_up = bell_draw(streams_of[5], (EXPERTS, D, FF), D ** -0.5, 0.125, ((0, 64), (1, 4)))
    w_down = bell_draw(streams_of[6], (EXPERTS, FF, D), FF ** -0.5, 0.21875, ((0, 64), (2, 4)))
    return {"tokens": tokens, "expert_ids": expert_ids, "gate_probs": gate_probs, "grad_out": grad_out, "w_gate": w_gate, "w_up": w_up, "w_down": w_down}


def silu_parts(gate_vals):
    sig_vals = jax.nn.sigmoid(gate_vals)
    return gate_vals * sig_vals, sig_vals * (1.0 + gate_vals * (1.0 - sig_vals))


def contract(left_side, right_side, left_dim, right_dim):
    return lax.dot_general(left_side, right_side, (((left_dim,), (right_dim,)), ((), ())), preferred_element_type=jnp.float32)


def expert_work(rows_in, grad_rows, gate_full, up_full, down_full):
    gate_vals = contract(rows_in, gate_full, 1, 0)
    up_vals = contract(rows_in, up_full, 1, 0)
    act_vals, slope_vals = silu_parts(gate_vals)
    hidden = (act_vals * up_vals).astype(jnp.bfloat16)
    expert_out = contract(hidden, down_full, 1, 0).astype(jnp.bfloat16)
    grad_hidden = contract(grad_rows, down_full, 1, 1)
    grad_gate_pre = (grad_hidden * up_vals * slope_vals).astype(jnp.bfloat16)
    grad_up_pre = (grad_hidden * act_vals).astype(jnp.bfloat16)
    grad_pair = (contract(grad_gate_pre, gate_full, 1, 1) + contract(grad_up_pre, up_full, 1, 1)).astype(jnp.bfloat16)
    grad_gate_w = contract(rows_in, grad_gate_pre, 0, 0).astype(jnp.bfloat16)
    grad_up_w = contract(rows_in, grad_up_pre, 0, 0).astype(jnp.bfloat16)
    grad_down_w = contract(hidden, grad_rows, 0, 0).astype(jnp.bfloat16)
    return expert_out, grad_pair, grad_gate_w, grad_up_w, grad_down_w


def reference(tokens, expert_ids, gate_probs, grad_out, w_gate, w_up, w_down):
    pair_count = TOKENS * TOP
    capacity = N_DP * N_EXPERT * MOST
    flat_ids = expert_ids.reshape(-1).astype(jnp.int32)
    flat_probs = gate_probs.reshape(-1)
    sorted_pairs = jnp.argsort(flat_ids, stable=True).astype(jnp.int32)
    counts = jnp.sum((flat_ids[None, :] == jnp.arange(EXPERTS, dtype=jnp.int32)[:, None]).astype(jnp.int32), axis=1).astype(jnp.int32)
    starts = (jnp.cumsum(counts) - counts).astype(jnp.int32)
    padded = jnp.concatenate([sorted_pairs, jnp.zeros((capacity,), jnp.int32)])

    def per_expert(inputs):
        expert, gate_full, up_full, down_full = inputs
        order_index = lax.dynamic_slice(padded, (starts[expert],), (capacity,)).astype(jnp.int32)
        is_live = jnp.arange(capacity, dtype=jnp.int32) < counts[expert]
        token_row = (order_index // TOP).astype(jnp.int32)
        rows_in = jnp.where(is_live[:, None], tokens[token_row], jnp.zeros((), tokens.dtype))
        weight = jnp.where(is_live, flat_probs[order_index], jnp.zeros((), flat_probs.dtype))
        grad_rows = (weight[:, None] * grad_out[token_row].astype(jnp.float32)).astype(jnp.bfloat16)
        results = expert_work(rows_in, grad_rows, gate_full, up_full, down_full)
        target = jnp.where(is_live, order_index, pair_count).astype(jnp.int32)
        return results + (target,)

    expert_out, grad_pair, grad_gate, grad_up, grad_down, target = lax.map(
        per_expert, (jnp.arange(EXPERTS, dtype=jnp.int32), w_gate, w_up, w_down))
    target = target.reshape(-1)
    out_flat = jnp.zeros((pair_count + 1, D), expert_out.dtype).at[target].set(expert_out.reshape(-1, D))[:pair_count]
    pair_flat = jnp.zeros((pair_count + 1, D), grad_pair.dtype).at[target].set(grad_pair.reshape(-1, D))[:pair_count]
    out_pairs = out_flat.reshape(TOKENS, TOP, D).astype(jnp.float32)
    layer_out = jnp.sum(out_pairs * gate_probs[:, :, None], axis=1).astype(jnp.bfloat16)
    grad_probs = jnp.sum(out_pairs * grad_out[:, None, :].astype(jnp.float32), axis=2)
    grad_tokens = jnp.sum(pair_flat.reshape(TOKENS, TOP, D).astype(jnp.float32), axis=1).astype(jnp.bfloat16)
    return layer_out, grad_tokens, grad_probs, grad_gate, grad_up, grad_down
```

```python
import jax
import jax.numpy as jnp
import numpy as np
from jax import lax
from jax.experimental import pallas as pl
from jax.experimental.pallas import tpu as pltpu
from jax.sharding import PartitionSpec as P

BF = jnp.bfloat16
F32 = jnp.float32
SLOTS = 8
META = 128
XC_PLANES = [[x * 16 + z * 2 + c for x in range(4) for c in range(2)] for z in range(8)]


def dot(left_side, right_side, left_dim, right_dim, precision=None):
    return lax.dot_general(
        left_side,
        right_side,
        (((left_dim,), (right_dim,)), ((), ())),
        precision=precision,
        preferred_element_type=F32,
    )


def along_z(value, way, cores=(0, 1)):
    pairs = []
    for i in range(lax.axis_size("expert")):
        step = way if i % 2 == 0 else -way
        if i % 2 in cores:
            pairs.append((i, i // 16 * 16 + (i % 16 // 2 + step) % 8 * 2 + i % 2))
    return lax.ppermute(value, "expert", pairs)


def other_core(value):
    return lax.ppermute(value, "expert", [(i, i ^ 1) for i in range(lax.axis_size("expert"))])


def gather_z(mine, first):
    own = jnp.concatenate([mine, other_core(mine)], axis=0)
    one = along_z(own, 1)
    two = along_z(one, 1)
    three = along_z(two, 1)
    four = along_z(three, 1, (1,))
    return jnp.concatenate([jnp.where(first, own, four), one, two, three], axis=0)


def scatter_z(partial, first):
    rows = partial.shape[0] // 4

    def block(i):
        return partial[i * rows : (i + 1) * rows]

    moved = along_z(block(0).astype(BF), -1, (1,))
    for i in (3, 2, 1):
        moved = along_z((block(i) + moved.astype(F32)).astype(BF), -1)
    total = moved.astype(F32) + jnp.where(first, block(0), 0.0)
    half = rows // 2
    return total[:half] + other_core(total[half:].astype(BF)).astype(F32)


def swap_rows(value):
    return lax.all_to_all(value, "expert", 0, 0, axis_index_groups=XC_PLANES, tiled=True)


def copies(pairs, sems):
    started = [
        pltpu.make_async_copy(source, target, sems.at[i])
        for i, (source, target) in enumerate(pairs)
    ]
    for copy in started:
        copy.start()
    return started


def pack_kernel(gate, up, down, out):
    width = gate.shape[1]
    out[:, :width] = gate[...]
    out[:, width : 2 * width] = up[...]
    out[:, 2 * width :] = down[...].astype(F32).T.astype(BF)


def unpack_kernel(packed, gate, up, down):
    width = gate.shape[1]
    gate[...] = packed[:, :width]
    up[...] = packed[:, width : 2 * width]
    down[...] = packed[:, 2 * width :].astype(F32).T.astype(BF)


def expert_kernel(
    rows, weights, out, pre, sums, rows_v, gate_up_v, down_v, pre_v, hidden, sums_v, sems
):
    part, hidden_width = down_v.shape[1:]
    both = 2 * hidden_width
    pairs = []
    for j in range(4):
        pairs += [
            (rows.at[:, j * part : (j + 1) * part], rows_v.at[j]),
            (weights.at[j, :, :both], gate_up_v.at[j]),
        ]
    for j in range(4):
        pairs += [
            (rows.at[:, (4 + j) * part : (5 + j) * part], rows_v.at[4 + j]),
            (weights.at[j, :, both:], down_v.at[j]),
        ]
    moves = copies(pairs, sems)
    for j in range(4):
        moves[2 * j].wait()
        moves[2 * j + 1].wait()
        product = dot(rows_v[j], gate_up_v[j], 1, 0)
        pre_v[...] = product if j == 0 else pre_v[...] + product
    for move in moves[8:]:
        move.wait()
    step = 128
    for i in range(0, pre_v.shape[0], step):
        at = slice(i, i + step)
        gate_vals, up_vals = pre_v[at, :hidden_width], pre_v[at, hidden_width:]
        sig_vals = 1.0 / (1.0 + jnp.exp(-gate_vals))
        act_vals = gate_vals * sig_vals
        hidden[at] = (act_vals * up_vals).astype(BF)
        grad_hidden = sum(dot(rows_v[4 + j, at], down_v[j], 1, 0) for j in range(4))
        slope_vals = sig_vals * (1.0 + gate_vals * (1.0 - sig_vals))
        pre[at, :hidden_width] = (grad_hidden * up_vals * slope_vals).astype(BF)
        pre[at, hidden_width:] = (grad_hidden * act_vals).astype(BF)
    outs = []
    for j in range(4):
        sums_v[j, :, :both] = dot(rows_v[j], pre[...], 0, 0).astype(BF)
        sums_v[j, :, both:] = dot(rows_v[4 + j], hidden[...], 0, 0).astype(BF)
        outs.append(
            pltpu.make_async_copy(
                sums_v.at[j], sums.at[j * part : (j + 1) * part], sems.at[16 + j]
            )
        )
        outs[-1].start()
    for j in range(4):
        out[:, j * part : (j + 1) * part] = dot(hidden[...], down_v[j], 1, 1).astype(BF)
    for move in outs:
        move.wait()


def pair_kernel(pre, weights, out, gate_up_v, sems):
    part, gate_up = gate_up_v.shape[1:]
    moves = copies([(weights.at[j, :, :gate_up], gate_up_v.at[j]) for j in range(4)], sems)
    for j in range(4):
        moves[j].wait()
        out[:, j * part : (j + 1) * part] = dot(pre[...], gate_up_v[j], 1, 1).astype(BF)


ANY = pl.BlockSpec(memory_space=pl.ANY)
VMEM = pl.BlockSpec(memory_space=pltpu.VMEM)


def call(kernel, in_specs, out_specs, outs, scratch=(), sems=0):
    held = [pltpu.VMEM(*shape) for shape in scratch]
    return pl.pallas_call(
        kernel,
        in_specs=in_specs,
        out_specs=out_specs,
        out_shape=[jax.ShapeDtypeStruct(*out) for out in outs],
        scratch_shapes=held + [pltpu.SemaphoreType.DMA((sems,))] * (sems > 0),
        compiler_params=pltpu.CompilerParams(vmem_limit_bytes=44 * 2**20),
        cost_estimate=pl.CostEstimate(flops=1, transcendentals=0, bytes_accessed=1),
    )


def pack(gate, up, down):
    rows, width = gate.shape
    step = rows // 4
    return pl.pallas_call(
        pack_kernel,
        grid=(4,),
        in_specs=[
            pl.BlockSpec((step, width), lambda i: (i, 0)),
            pl.BlockSpec((step, width), lambda i: (i, 0)),
            pl.BlockSpec((width, step), lambda i: (0, i)),
        ],
        out_specs=pl.BlockSpec((step, 3 * width), lambda i: (i, 0)),
        out_shape=jax.ShapeDtypeStruct((rows, 3 * width), BF),
    )(gate, up, down)


def unpack(packed):
    rows, width = packed.shape[0], packed.shape[1] // 3
    step = rows // 4
    return pl.pallas_call(
        unpack_kernel,
        grid=(4,),
        in_specs=[pl.BlockSpec((step, 3 * width), lambda i: (i, 0))],
        out_specs=[
            pl.BlockSpec((step, width), lambda i: (i, 0)),
            pl.BlockSpec((step, width), lambda i: (i, 0)),
            pl.BlockSpec((width, step), lambda i: (0, i)),
        ],
        out_shape=[
            jax.ShapeDtypeStruct((rows, width), BF),
            jax.ShapeDtypeStruct((rows, width), BF),
            jax.ShapeDtypeStruct((width, rows), BF),
        ],
    )(packed)


def pieces(value):
    high = lax.reduce_precision(value, 8, 7)
    mid = lax.reduce_precision(value - high, 8, 7)
    return high, mid, value - high - mid


def body(tokens, expert_ids, gate_probs, grad_out, w_gate, w_up, w_down):
    me = lax.axis_index("expert")
    z, first = me % 16 // 2, me % 2 == 0
    rows, width = tokens.shape
    top = expert_ids.shape[1]
    hidden_width = w_gate.shape[2]
    part = width // 4
    count = 8
    held = count * rows

    experts = lax.all_gather(pack(w_gate[0], w_up[0], w_down[0]), "dp")

    meta = jnp.concatenate(
        [expert_ids.astype(F32), *pieces(gate_probs), jnp.zeros((rows, META - 4 * top), F32)],
        axis=1,
    ).astype(BF)
    sources = gather_z(jnp.concatenate([tokens, grad_out, meta], axis=1), first)
    meta = sources[:, 2 * width :].astype(F32)
    sources = sources[:, : 2 * width]

    group = jnp.arange(8, dtype=jnp.int32)
    dest = (group // 2 * 16 + z * 2 + group % 2).astype(F32)[None, :]
    match = [meta[:, k : k + 1] == dest for k in range(top)]
    probs = meta[:, top : 2 * top] + meta[:, 2 * top : 3 * top] + meta[:, 3 * top : 4 * top]
    holds = sum(hit.astype(F32) for hit in match)
    weight = sum(jnp.where(hit, probs[:, k : k + 1], 0.0) for k, hit in enumerate(match))
    token_id = np.arange(held)
    slot_id = np.arange(8 * count * SLOTS)
    earlier = (token_id[None, :] < token_id[:, None]) & (
        token_id[None, :] // rows == token_id[:, None] // rows
    )
    spread = jnp.asarray(slot_id[None, :] // (count * SLOTS) == np.arange(8)[:, None], F32)
    rank = dot(jnp.asarray(earlier, BF), holds.astype(BF), 1, 0)
    rank = dot(jnp.where(holds > 0, rank, -1.0).astype(BF), spread.astype(BF), 1, 0)
    wanted = np.where(
        slot_id[None, :] // SLOTS % count == token_id[:, None] // rows, slot_id[None, :] % SLOTS, -2
    )
    fills = rank == jnp.asarray(wanted, F32)
    select = fills.astype(BF)
    weights = jnp.where(fills, dot(weight, spread, 1, 0, lax.Precision.HIGHEST), 0.0)
    slot_weight = dot(weights, jnp.ones((held, 1), F32), 0, 0, lax.Precision.HIGHEST)

    scale = jnp.where(jnp.arange(2 * width)[None, :] < width, 1.0, slot_weight)
    arrived = swap_rows((dot(select, sources, 0, 0) * scale).astype(BF))

    slots = arrived.shape[0]
    wide = (slots, 2 * hidden_width)
    expert_out, grad_pre, sums = call(
        expert_kernel,
        [ANY] * 2,
        [VMEM, VMEM, ANY],
        [((slots, width), BF), (wide, BF), ((width, 3 * hidden_width), BF)],
        [
            ((8, slots, part), BF),
            ((4, part, 2 * hidden_width), BF),
            ((4, part, hidden_width), BF),
            (wide, F32),
            ((slots, hidden_width), BF),
            ((4, part, 3 * hidden_width), BF),
        ],
        20,
    )(arrived, experts)
    weight_grads = lax.psum_scatter(sums, "dp", scatter_dimension=0, tiled=True)
    back_out = swap_rows(expert_out)
    (grad_pair,) = call(
        pair_kernel,
        [VMEM, ANY],
        [VMEM],
        [((slots, width), BF)],
        [((4, part, 2 * hidden_width), BF)],
        4,
    )(grad_pre, experts)

    back_grads = swap_rows(grad_pair)
    weight_high, weight_mid, _ = pieces(weights)
    layer_part = dot(weight_high.astype(BF), back_out, 1, 0) + dot(
        weight_mid.astype(BF), back_out, 1, 0
    )
    products = jnp.where(fills, dot(sources[:, width:], back_out, 1, 1), 0.0)
    products = dot(products, spread, 1, 1, lax.Precision.HIGHEST)
    prob_part = jnp.concatenate(
        [jnp.sum(jnp.where(hit, products, 0.0), axis=1, keepdims=True) for hit in match], axis=1
    )
    prob_part = jnp.concatenate(
        [*pieces(prob_part), jnp.zeros((held, META - 3 * top), F32)], axis=1
    )
    layer_sum = scatter_z(jnp.concatenate([layer_part, prob_part], axis=1), first)
    grad_tokens = scatter_z(dot(select, back_grads, 1, 0), first).astype(BF)
    layer_out = layer_sum[:, :width].astype(BF)
    prob_sum = layer_sum[:, width:]
    grad_probs = prob_sum[:, :top] + prob_sum[:, top : 2 * top] + prob_sum[:, 2 * top : 3 * top]
    grad_gate, grad_up, grad_down = unpack(weight_grads)
    return layer_out, grad_tokens, grad_probs, grad_gate[None], grad_up[None], grad_down[None]


def solution(mesh):
    return jax.shard_map(
        body,
        mesh=mesh,
        in_specs=(
            P(("dp", "expert"), None),
            P(("dp", "expert"), None),
            P(("dp", "expert"), None),
            P(("dp", "expert"), None),
            P("expert", "dp", None),
            P("expert", "dp", None),
            P("expert", None, "dp"),
        ),
        out_specs=(
            P(("dp", "expert"), None),
            P(("dp", "expert"), None),
            P(("dp", "expert"), None),
            P("expert", "dp", None),
            P("expert", "dp", None),
            P("expert", None, "dp"),
        ),
        check_vma=False,
    )
```

```python
import jax
import jax.numpy as jnp
import numpy as np
from jax import lax
from jax.experimental import pallas as pl
from jax.experimental.pallas import tpu as pltpu
from jax.sharding import PartitionSpec as P

BF = jnp.bfloat16
F32 = jnp.float32
SLOTS = 8
META = 128
XC_PLANES = [[x * 16 + z * 2 + c for x in range(4) for c in range(2)] for z in range(8)]


def dot(left_side, right_side, left_dim, right_dim, precision=None):
    return lax.dot_general(
        left_side,
        right_side,
        (((left_dim,), (right_dim,)), ((), ())),
        precision=precision,
        preferred_element_type=F32,
    )


def along_z(value, way, cores=(0, 1)):
    pairs = []
    for i in range(lax.axis_size("expert")):
        step = way if i % 2 == 0 else -way
        if i % 2 in cores:
            pairs.append((i, i // 16 * 16 + (i % 16 // 2 + step) % 8 * 2 + i % 2))
    return lax.ppermute(value, "expert", pairs)


def other_core(value):
    return lax.ppermute(value, "expert", [(i, i ^ 1) for i in range(lax.axis_size("expert"))])


def gather_z(mine, first):
    own = jnp.concatenate([mine, other_core(mine)], axis=0)
    one = along_z(own, 1)
    two = along_z(one, 1)
    three = along_z(two, 1)
    four = along_z(three, 1, (1,))
    return jnp.concatenate([jnp.where(first, own, four), one, two, three], axis=0)


def scatter_z(partial, first):
    rows = partial.shape[0] // 4

    def block(i):
        return partial[i * rows : (i + 1) * rows]

    moved = along_z(block(0).astype(BF), -1, (1,))
    for i in (3, 2, 1):
        moved = along_z((block(i) + moved.astype(F32)).astype(BF), -1)
    total = moved.astype(F32) + jnp.where(first, block(0), 0.0)
    half = rows // 2
    return total[:half] + other_core(total[half:].astype(BF)).astype(F32)


def swap_rows(value):
    return lax.all_to_all(value, "expert", 0, 0, axis_index_groups=XC_PLANES, tiled=True)


def copies(pairs, sems):
    started = [
        pltpu.make_async_copy(source, target, sems.at[i])
        for i, (source, target) in enumerate(pairs)
    ]
    for copy in started:
        copy.start()
    return started


def pack_kernel(gate, up, down, out):
    width = gate.shape[1]
    out[:, :width] = gate[...]
    out[:, width : 2 * width] = up[...]
    out[:, 2 * width :] = down[...].T


def unpack_kernel(packed, gate, up, down):
    width = gate.shape[1]
    gate[...] = packed[:, :width]
    up[...] = packed[:, width : 2 * width]
    down[...] = packed[:, 2 * width :].T


def expert_kernel(
    rows, weights, out, pair, sums, rows_v, gate_up_v, down_v, pre_v, hidden, pre, sums_v, sems
):
    part, hidden_width = down_v.shape[1:]
    both = 2 * hidden_width
    pairs = []
    for j in range(4):
        pairs += [
            (rows.at[:, j * part : (j + 1) * part], rows_v.at[j]),
            (weights.at[j, :, :both], gate_up_v.at[j]),
        ]
    for j in range(4):
        pairs += [
            (rows.at[:, (4 + j) * part : (5 + j) * part], rows_v.at[4 + j]),
            (weights.at[j, :, both:], down_v.at[j]),
        ]
    moves = copies(pairs, sems)
    for j in range(4):
        moves[2 * j].wait()
        moves[2 * j + 1].wait()
        product = dot(rows_v[j], gate_up_v[j], 1, 0)
        pre_v[...] = product if j == 0 else pre_v[...] + product
    for move in moves[8:]:
        move.wait()
    step = 128
    for i in range(0, pre_v.shape[0], step):
        at = slice(i, i + step)
        gate_vals, up_vals = pre_v[at, :hidden_width], pre_v[at, hidden_width:]
        sig_vals = 1.0 / (1.0 + jnp.exp(-gate_vals))
        act_vals = gate_vals * sig_vals
        hidden[at] = (act_vals * up_vals).astype(BF)
        grad_hidden = sum(dot(rows_v[4 + j, at], down_v[j], 1, 0) for j in range(4))
        slope_vals = sig_vals * (1.0 + gate_vals * (1.0 - sig_vals))
        pre[at, :hidden_width] = (grad_hidden * up_vals * slope_vals).astype(BF)
        pre[at, hidden_width:] = (grad_hidden * act_vals).astype(BF)
    outs = []
    for j in range(4):
        sums_v[j, :, :both] = dot(rows_v[j], pre[...], 0, 0).astype(BF)
        sums_v[j, :, both:] = dot(rows_v[4 + j], hidden[...], 0, 0).astype(BF)
        outs.append(
            pltpu.make_async_copy(
                sums_v.at[j], sums.at[j * part : (j + 1) * part], sems.at[16 + j]
            )
        )
        outs[-1].start()
    for j in range(4):
        at = slice(j * part, (j + 1) * part)
        pair[:, at] = dot(pre[...], gate_up_v[j], 1, 1).astype(BF)
        out[:, at] = dot(hidden[...], down_v[j], 1, 1).astype(BF)
    for move in outs:
        move.wait()


def combine_kernel(back, sources, weights, select, place, out, back_v, cot_v, sems):
    width = back.shape[1]
    moves = copies([(back, back_v), (sources.at[:, width : 2 * width], cot_v)], sems)
    high = weights[...].astype(BF)
    mid = (weights[...] - high.astype(F32)).astype(BF)
    moves[0].wait()
    out[:, :width] = dot(high, back_v[...], 1, 0) + dot(mid, back_v[...], 1, 0)
    moves[1].wait()
    products = dot(cot_v[...], back_v[...], 1, 1) * select[...].astype(F32)
    group = dot(products, place[...], 1, 0, lax.Precision.HIGHEST)
    high = group.astype(BF).astype(F32)
    lane = lax.broadcasted_iota(jnp.int32, group.shape, 1)
    out[:, width:] = jnp.where(lane < group.shape[1] // 2, high, group - high)


ANY = pl.BlockSpec(memory_space=pl.ANY)
VMEM = pl.BlockSpec(memory_space=pltpu.VMEM)


def call(kernel, in_specs, out_specs, outs, scratch, sems, limit):
    return pl.pallas_call(
        kernel,
        in_specs=in_specs,
        out_specs=out_specs,
        out_shape=[jax.ShapeDtypeStruct(*out) for out in outs],
        scratch_shapes=[*(pltpu.VMEM(*held) for held in scratch), pltpu.SemaphoreType.DMA((sems,))],
        compiler_params=pltpu.CompilerParams(vmem_limit_bytes=limit * 2**20),
        cost_estimate=pl.CostEstimate(flops=1, transcendentals=0, bytes_accessed=1),
    )


def pack(gate, up, down):
    rows, width = gate.shape
    step = rows // 4
    return pl.pallas_call(
        pack_kernel,
        grid=(4,),
        in_specs=[
            pl.BlockSpec((step, width), lambda i: (i, 0)),
            pl.BlockSpec((step, width), lambda i: (i, 0)),
            pl.BlockSpec((width, step), lambda i: (0, i)),
        ],
        out_specs=pl.BlockSpec((step, 3 * width), lambda i: (i, 0)),
        out_shape=jax.ShapeDtypeStruct((rows, 3 * width), BF),
    )(gate, up, down)


def unpack(packed):
    rows, width = packed.shape[0], packed.shape[1] // 3
    step = rows // 4
    return pl.pallas_call(
        unpack_kernel,
        grid=(4,),
        in_specs=[pl.BlockSpec((step, 3 * width), lambda i: (i, 0))],
        out_specs=[
            pl.BlockSpec((step, width), lambda i: (i, 0)),
            pl.BlockSpec((step, width), lambda i: (i, 0)),
            pl.BlockSpec((width, step), lambda i: (0, i)),
        ],
        out_shape=[
            jax.ShapeDtypeStruct((rows, width), BF),
            jax.ShapeDtypeStruct((rows, width), BF),
            jax.ShapeDtypeStruct((width, rows), BF),
        ],
    )(packed)


def pieces(value):
    high = lax.reduce_precision(value, 8, 7)
    mid = lax.reduce_precision(value - high, 8, 7)
    return high, mid, value - high - mid


def body(tokens, expert_ids, gate_probs, grad_out, w_gate, w_up, w_down):
    me = lax.axis_index("expert")
    z, first = me % 16 // 2, me % 2 == 0
    rows, width = tokens.shape
    top = expert_ids.shape[1]
    hidden_width = w_gate.shape[2]
    part = width // 4
    count = 8
    held = count * rows

    experts = lax.all_gather(pack(w_gate[0], w_up[0], w_down[0]), "dp")

    meta = jnp.concatenate(
        [expert_ids.astype(F32), *pieces(gate_probs), jnp.zeros((rows, META - 4 * top), F32)],
        axis=1,
    ).astype(BF)
    gathered = gather_z(jnp.concatenate([tokens, grad_out, meta], axis=1), first)
    meta = gathered[:, 2 * width :].astype(F32)
    sources = gathered[:, : 2 * width]

    group = jnp.arange(8, dtype=jnp.int32)
    dest = (group // 2 * 16 + z * 2 + group % 2).astype(F32)[None, :]
    match = [meta[:, k : k + 1] == dest for k in range(top)]
    probs = meta[:, top : 2 * top] + meta[:, 2 * top : 3 * top] + meta[:, 3 * top : 4 * top]
    holds = sum(hit.astype(F32) for hit in match)
    weight = sum(jnp.where(hit, probs[:, k : k + 1], 0.0) for k, hit in enumerate(match))
    token_id = np.arange(held)
    slot_id = np.arange(8 * count * SLOTS)
    earlier = (token_id[None, :] < token_id[:, None]) & (
        token_id[None, :] // rows == token_id[:, None] // rows
    )
    spread = jnp.asarray(slot_id[None, :] // (count * SLOTS) == np.arange(8)[:, None], F32)
    rank = dot(jnp.asarray(earlier, BF), holds.astype(BF), 1, 0)
    rank = dot(jnp.where(holds > 0, rank, -1.0).astype(BF), spread.astype(BF), 1, 0)
    wanted = np.where(
        slot_id[None, :] // SLOTS % count == token_id[:, None] // rows, slot_id[None, :] % SLOTS, -2
    )
    fills = rank == jnp.asarray(wanted, F32)
    select = fills.astype(BF)
    weights = jnp.where(fills, dot(weight, spread, 1, 0, lax.Precision.HIGHEST), 0.0)
    slot_weight = dot(weights, jnp.ones((held, 1), F32), 0, 0, lax.Precision.HIGHEST)

    scale = jnp.where(jnp.arange(2 * width)[None, :] < width, 1.0, slot_weight)
    arrived = swap_rows((dot(select, sources, 0, 0) * scale).astype(BF))

    slots = arrived.shape[0]
    wide = (slots, 2 * hidden_width)
    expert_out, grad_pair, sums = call(
        expert_kernel,
        [ANY] * 2,
        [VMEM, VMEM, ANY],
        [((slots, width), BF), ((slots, width), BF), ((width, 3 * hidden_width), BF)],
        [
            ((8, slots, part), BF),
            ((4, part, 2 * hidden_width), BF),
            ((4, part, hidden_width), BF),
            (wide, F32),
            ((slots, hidden_width), BF),
            (wide, BF),
            ((4, part, 3 * hidden_width), BF),
        ],
        20,
        56,
    )(arrived, experts)
    weight_grads = lax.psum_scatter(sums, "dp", scatter_dimension=0, tiled=True)

    back_grads = swap_rows(grad_pair)
    expert_out, back_grads = lax.optimization_barrier((expert_out, back_grads))
    back_out = swap_rows(expert_out)
    lane = jnp.arange(META, dtype=jnp.int32)[None, :] % (META // 2)
    place = (lane == z * 8 + jnp.asarray(slot_id // (count * SLOTS), jnp.int32)[:, None]).astype(F32)
    (layer_part,) = call(
        combine_kernel,
        [ANY, ANY, VMEM, VMEM, VMEM],
        [VMEM],
        [((held, width + META), F32)],
        [((slots, width), BF), ((held, width), BF)],
        2,
        32,
    )(back_out, gathered, weights, select, place)
    layer_sum = scatter_z(layer_part, first)
    grad_tokens = scatter_z(dot(select, back_grads, 1, 0), first).astype(BF)
    layer_out = layer_sum[:, :width].astype(BF)
    prob_sum = layer_sum[:, width : width + META // 2] + layer_sum[:, width + META // 2 :]
    named = expert_ids % 16 // 2 * 8 + expert_ids // 16 * 2 + expert_ids % 2
    named = named[:, :, None] == jnp.arange(META // 2, dtype=jnp.int32)
    grad_probs = jnp.sum(jnp.where(named, prob_sum[:, None, :], 0.0), axis=2)
    grad_gate, grad_up, grad_down = unpack(weight_grads)
    return layer_out, grad_tokens, grad_probs, grad_gate[None], grad_up[None], grad_down[None]


def solution(mesh):
    return jax.shard_map(
        body,
        mesh=mesh,
        in_specs=(
            P(("dp", "expert"), None),
            P(("dp", "expert"), None),
            P(("dp", "expert"), None),
            P(("dp", "expert"), None),
            P("expert", "dp", None),
            P("expert", "dp", None),
            P("expert", None, "dp"),
        ),
        out_specs=(
            P(("dp", "expert"), None),
            P(("dp", "expert"), None),
            P(("dp", "expert"), None),
            P("expert", "dp", None),
            P("expert", "dp", None),
            P("expert", None, "dp"),
        ),
        check_vma=False,
    )
```

```python
import jax
import jax.numpy as jnp
import numpy as np
from jax import lax
from jax.experimental import pallas as pl
from jax.experimental.pallas import tpu as pltpu
from jax.sharding import PartitionSpec as P

BF = jnp.bfloat16
F32 = jnp.float32
SLOTS = 8
META = 128
XC_PLANES = [[x * 16 + z * 2 + c for x in range(4) for c in range(2)] for z in range(8)]


def dot(left_side, right_side, left_dim, right_dim, precision=None):
    return lax.dot_general(
        left_side,
        right_side,
        (((left_dim,), (right_dim,)), ((), ())),
        precision=precision,
        preferred_element_type=F32,
    )


def along_z(value, way, cores=(0, 1)):
    pairs = []
    for i in range(lax.axis_size("expert")):
        step = way if i % 2 == 0 else -way
        if i % 2 in cores:
            pairs.append((i, i // 16 * 16 + (i % 16 // 2 + step) % 8 * 2 + i % 2))
    return lax.ppermute(value, "expert", pairs)


def other_core(value):
    return lax.ppermute(value, "expert", [(i, i ^ 1) for i in range(lax.axis_size("expert"))])


def gather_z(mine, first):
    own = jnp.concatenate([mine, other_core(mine)], axis=0)
    one = along_z(own, 1)
    two = along_z(one, 1)
    three = along_z(two, 1)
    four = along_z(three, 1, (1,))
    return jnp.concatenate([jnp.where(first, own, four), one, two, three], axis=0)


def scatter_z(partial, first):
    rows = partial.shape[0] // 4

    def block(i):
        return partial[i * rows : (i + 1) * rows]

    moved = along_z(block(0).astype(BF), -1, (1,))
    for i in (3, 2, 1):
        moved = along_z((block(i) + moved.astype(F32)).astype(BF), -1)
    total = moved.astype(F32) + jnp.where(first, block(0), 0.0)
    half = rows // 2
    return total[:half] + other_core(total[half:].astype(BF)).astype(F32)


def swap_rows(value):
    return lax.all_to_all(value, "expert", 0, 0, axis_index_groups=XC_PLANES, tiled=True)


def copies(pairs, sems):
    started = [
        pltpu.make_async_copy(source, target, sems.at[i])
        for i, (source, target) in enumerate(pairs)
    ]
    for copy in started:
        copy.start()
    return started


def pack_moves(gate, up, down, packed):
    rows, width = gate.shape
    rest = width - rows
    at = 2 * width + rows
    return [
        (gate, packed.at[:, :width]),
        (up, packed.at[:, width : 2 * width]),
        (down.at[:rows], packed.at[:, 2 * width : at]),
        (down.at[rows:, :rest], packed.at[:rest, at:]),
        (down.at[rows:, rest:], packed.at[rest:, at:]),
    ]


def pack_kernel(gate, up, down, packed, sems):
    for move in copies(pack_moves(gate, up, down, packed), sems):
        move.wait()


def unpack_kernel(packed, gate, up, down, sems):
    moves = [(source, target) for target, source in pack_moves(gate, up, down, packed)]
    for move in copies(moves, sems):
        move.wait()


def expert_kernel(
    rows, weights, out, pair, sums, rows_v, gate_up_v, down_v, pre_v, grad_v, hidden, pre, sums_v,
    out_v, pair_v, sems
):
    part, rest = down_v.shape[2], down_v.shape[1] - down_v.shape[2]
    hidden_width = down_v.shape[1]
    both = 2 * hidden_width
    last = both + part
    pairs = []
    for j in range(4):
        pairs += [
            (rows.at[:, j * part : (j + 1) * part], rows_v.at[j]),
            (weights.at[j, :, :both], gate_up_v.at[j]),
        ]
    for j in range(4):
        pairs += [
            (rows.at[:, (4 + j) * part : (5 + j) * part], rows_v.at[4 + j]),
            (weights.at[j, :, both:last], down_v.at[j, :part]),
            (weights.at[j, :rest, last:], down_v.at[j, part:, :rest]),
            (weights.at[j, rest:, last:], down_v.at[j, part:, rest:]),
        ]
    moves = copies(pairs, sems)
    for j in range(4):
        moves[2 * j].wait()
        moves[2 * j + 1].wait()
        product = dot(rows_v[j], gate_up_v[j], 1, 0)
        pre_v[...] = product if j == 0 else pre_v[...] + product
    for j in range(4):
        for move in moves[8 + 4 * j : 12 + 4 * j]:
            move.wait()
        product = dot(rows_v[4 + j], down_v[j], 1, 1)
        grad_v[...] = product if j == 0 else grad_v[...] + product
    step = 128
    for i in range(0, pre_v.shape[0], step):
        at = slice(i, i + step)
        gate_vals, up_vals = pre_v[at, :hidden_width], pre_v[at, hidden_width:]
        sig_vals = 1.0 / (1.0 + jnp.exp(-gate_vals))
        act_vals = gate_vals * sig_vals
        hidden[at] = (act_vals * up_vals).astype(BF)
        slope_vals = sig_vals * (1.0 + gate_vals * (1.0 - sig_vals))
        pre[at, :hidden_width] = (grad_v[at] * up_vals * slope_vals).astype(BF)
        pre[at, hidden_width:] = (grad_v[at] * act_vals).astype(BF)
    outs = []

    def leave(source, target):
        outs.append(pltpu.make_async_copy(source, target, sems.at[len(moves) + len(outs)]))
        outs[-1].start()

    for j in range(4):
        sums_v[j, :, :both] = dot(rows_v[j], pre[...], 0, 0).astype(BF)
        down_sum = dot(hidden[...], rows_v[4 + j], 0, 0).astype(BF)
        sums_v[j, :, both:last] = down_sum[:part]
        sums_v[j, :rest, last:] = down_sum[part:, :rest]
        sums_v[j, rest:, last:] = down_sum[part:, rest:]
        leave(sums_v.at[j], sums.at[j * part : (j + 1) * part])
    for j in range(4):
        at = slice(j * part, (j + 1) * part)
        pair_v[j] = dot(pre[...], gate_up_v[j], 1, 1).astype(BF)
        leave(pair_v.at[j], pair.at[:, at])
        out_v[j] = dot(hidden[...], down_v[j], 1, 0).astype(BF)
        leave(out_v.at[j], out.at[:, at])
    for move in outs:
        move.wait()


def combine_kernel(back, sources, weights, select, place, out, back_v, cot_v, sems):
    width = back.shape[1]
    moves = copies([(back, back_v), (sources.at[:, width : 2 * width], cot_v)], sems)
    high = weights[...].astype(BF)
    mid = (weights[...] - high.astype(F32)).astype(BF)
    moves[0].wait()
    out[:, :width] = dot(high, back_v[...], 1, 0) + dot(mid, back_v[...], 1, 0)
    moves[1].wait()
    products = dot(cot_v[...], back_v[...], 1, 1) * select[...].astype(F32)
    group = dot(products, place[...], 1, 0, lax.Precision.HIGHEST)
    high = group.astype(BF).astype(F32)
    lane = lax.broadcasted_iota(jnp.int32, group.shape, 1)
    out[:, width:] = jnp.where(lane < group.shape[1] // 2, high, group - high)


ANY = pl.BlockSpec(memory_space=pl.ANY)
VMEM = pl.BlockSpec(memory_space=pltpu.VMEM)


def call(kernel, in_specs, out_specs, outs, scratch, sems, limit):
    return pl.pallas_call(
        kernel,
        in_specs=in_specs,
        out_specs=out_specs,
        out_shape=[jax.ShapeDtypeStruct(*out) for out in outs],
        scratch_shapes=[*(pltpu.VMEM(*held) for held in scratch), pltpu.SemaphoreType.DMA((sems,))],
        compiler_params=pltpu.CompilerParams(vmem_limit_bytes=limit * 2**20),
        cost_estimate=pl.CostEstimate(flops=1, transcendentals=0, bytes_accessed=1),
    )


def pack(gate, up, down):
    rows, width = gate.shape
    return call(pack_kernel, [ANY] * 3, [VMEM], [((rows, 3 * width), BF)], [], 5, 16)(
        gate, up, down
    )[0]


def unpack(packed):
    rows, width = packed.shape[0], packed.shape[1] // 3
    outs = [((rows, width), BF), ((rows, width), BF), ((width, rows), BF)]
    return call(unpack_kernel, [VMEM], [ANY] * 3, outs, [], 5, 16)(packed)


def pieces(value):
    high = lax.reduce_precision(value, 8, 7)
    mid = lax.reduce_precision(value - high, 8, 7)
    return high, mid, value - high - mid


def body(tokens, expert_ids, gate_probs, grad_out, w_gate, w_up, w_down):
    me = lax.axis_index("expert")
    z, first = me % 16 // 2, me % 2 == 0
    rows, width = tokens.shape
    top = expert_ids.shape[1]
    hidden_width = w_gate.shape[2]
    part = width // 4
    count = 8
    held = count * rows

    experts = lax.all_gather(pack(w_gate[0], w_up[0], w_down[0]), "dp")

    meta = jnp.concatenate(
        [expert_ids.astype(F32), *pieces(gate_probs), jnp.zeros((rows, META - 4 * top), F32)],
        axis=1,
    ).astype(BF)
    gathered = gather_z(jnp.concatenate([tokens, grad_out, meta], axis=1), first)
    meta = gathered[:, 2 * width :].astype(F32)
    sources = gathered[:, : 2 * width]

    group = jnp.arange(8, dtype=jnp.int32)
    dest = (group // 2 * 16 + z * 2 + group % 2).astype(F32)[None, :]
    match = [meta[:, k : k + 1] == dest for k in range(top)]
    probs = meta[:, top : 2 * top] + meta[:, 2 * top : 3 * top] + meta[:, 3 * top : 4 * top]
    holds = sum(hit.astype(F32) for hit in match)
    weight = sum(jnp.where(hit, probs[:, k : k + 1], 0.0) for k, hit in enumerate(match))
    token_id = np.arange(held)
    slot_id = np.arange(8 * count * SLOTS)
    earlier = (token_id[None, :] < token_id[:, None]) & (
        token_id[None, :] // rows == token_id[:, None] // rows
    )
    spread = jnp.asarray(slot_id[None, :] // (count * SLOTS) == np.arange(8)[:, None], F32)
    rank = dot(jnp.asarray(earlier, BF), holds.astype(BF), 1, 0)
    rank = dot(jnp.where(holds > 0, rank, -1.0).astype(BF), spread.astype(BF), 1, 0)
    wanted = np.where(
        slot_id[None, :] // SLOTS % count == token_id[:, None] // rows, slot_id[None, :] % SLOTS, -2
    )
    fills = rank == jnp.asarray(wanted, F32)
    select = fills.astype(BF)
    weights = jnp.where(fills, dot(weight, spread, 1, 0, lax.Precision.HIGHEST), 0.0)
    slot_weight = dot(weights, jnp.ones((held, 1), F32), 0, 0, lax.Precision.HIGHEST)

    scale = jnp.where(jnp.arange(2 * width)[None, :] < width, 1.0, slot_weight)
    arrived = swap_rows((dot(select, sources, 0, 0) * scale).astype(BF))

    slots = arrived.shape[0]
    wide = (slots, 2 * hidden_width)
    expert_out, grad_pair, sums = call(
        expert_kernel,
        [ANY] * 2,
        [ANY, ANY, ANY],
        [((slots, width), BF), ((slots, width), BF), ((width, 3 * hidden_width), BF)],
        [
            ((8, slots, part), BF),
            ((4, part, 2 * hidden_width), BF),
            ((4, hidden_width, part), BF),
            (wide, F32),
            ((slots, hidden_width), F32),
            ((slots, hidden_width), BF),
            (wide, BF),
            ((4, part, 3 * hidden_width), BF),
            ((4, slots, part), BF),
            ((4, slots, part), BF),
        ],
        36,
        56,
    )(arrived, experts)
    weight_grads = lax.psum_scatter(sums, "dp", scatter_dimension=0, tiled=True)

    back_grads = swap_rows(grad_pair)
    expert_out, back_grads = lax.optimization_barrier((expert_out, back_grads))
    back_out = swap_rows(expert_out)
    lane = jnp.arange(META, dtype=jnp.int32)[None, :] % (META // 2)
    place = (lane == z * 8 + jnp.asarray(slot_id // (count * SLOTS), jnp.int32)[:, None]).astype(F32)
    (layer_part,) = call(
        combine_kernel,
        [ANY, ANY, VMEM, VMEM, VMEM],
        [VMEM],
        [((held, width + META), F32)],
        [((slots, width), BF), ((held, width), BF)],
        2,
        32,
    )(back_out, gathered, weights, select, place)
    layer_sum = scatter_z(layer_part, first)
    grad_tokens = scatter_z(dot(select, back_grads, 1, 0), first).astype(BF)
    layer_out = layer_sum[:, :width].astype(BF)
    prob_sum = layer_sum[:, width : width + META // 2] + layer_sum[:, width + META // 2 :]
    named = expert_ids % 16 // 2 * 8 + expert_ids // 16 * 2 + expert_ids % 2
    named = named[:, :, None] == jnp.arange(META // 2, dtype=jnp.int32)
    grad_probs = jnp.sum(jnp.where(named, prob_sum[:, None, :], 0.0), axis=2)
    grad_gate, grad_up, grad_down = unpack(weight_grads)
    return layer_out, grad_tokens, grad_probs, grad_gate[None], grad_up[None], grad_down[None]


def solution(mesh):
    return jax.shard_map(
        body,
        mesh=mesh,
        in_specs=(
            P(("dp", "expert"), None),
            P(("dp", "expert"), None),
            P(("dp", "expert"), None),
            P(("dp", "expert"), None),
            P("expert", "dp", None),
            P("expert", "dp", None),
            P("expert", None, "dp"),
        ),
        out_specs=(
            P(("dp", "expert"), None),
            P(("dp", "expert"), None),
            P(("dp", "expert"), None),
            P("expert", "dp", None),
            P("expert", "dp", None),
            P("expert", None, "dp"),
        ),
        check_vma=False,
    )
```

```python
import jax
import jax.numpy as jnp
import numpy as np
from jax import lax
from jax.experimental import pallas as pl
from jax.experimental.pallas import tpu as pltpu
from jax.sharding import PartitionSpec as P

BF = jnp.bfloat16
F32 = jnp.float32
SLOTS = 8
META = 128
XC_PLANES = [[x * 16 + z * 2 + c for x in range(4) for c in range(2)] for z in range(8)]


def dot(left_side, right_side, left_dim, right_dim, precision=None):
    return lax.dot_general(
        left_side,
        right_side,
        (((left_dim,), (right_dim,)), ((), ())),
        precision=precision,
        preferred_element_type=F32,
    )


def along_z(value, way, cores=(0, 1)):
    pairs = []
    for i in range(lax.axis_size("expert")):
        step = way if i % 2 == 0 else -way
        if i % 2 in cores:
            pairs.append((i, i // 16 * 16 + (i % 16 // 2 + step) % 8 * 2 + i % 2))
    return lax.ppermute(value, "expert", pairs)


def other_core(value):
    return lax.ppermute(value, "expert", [(i, i ^ 1) for i in range(lax.axis_size("expert"))])


def gather_z(mine, first):
    own = jnp.concatenate([mine, other_core(mine)], axis=0)
    one = along_z(own, 1)
    two = along_z(one, 1)
    three = along_z(two, 1)
    four = along_z(three, 1, (1,))
    return jnp.concatenate([jnp.where(first, own, four), one, two, three], axis=0)


def scatter_z(partial, first):
    rows = partial.shape[0] // 4

    def block(i):
        return partial[i * rows : (i + 1) * rows]

    moved = along_z(block(0).astype(BF), -1, (1,))
    for i in (3, 2, 1):
        moved = along_z((block(i) + moved.astype(F32)).astype(BF), -1)
    total = moved.astype(F32) + jnp.where(first, block(0), 0.0)
    half = rows // 2
    return total[:half] + other_core(total[half:].astype(BF)).astype(F32)


def swap_rows(value):
    return lax.all_to_all(value, "expert", 0, 0, axis_index_groups=XC_PLANES, tiled=True)


def copies(pairs, sems):
    started = [
        pltpu.make_async_copy(source, target, sems.at[i])
        for i, (source, target) in enumerate(pairs)
    ]
    for copy in started:
        copy.start()
    return started


def pack_moves(gate, up, down, packed):
    rows, width = gate.shape
    rest = width - rows
    at = 2 * width + rows
    return [
        (gate, packed.at[:, :width]),
        (up, packed.at[:, width : 2 * width]),
        (down.at[:rows], packed.at[:, 2 * width : at]),
        (down.at[rows:, :rest], packed.at[:rest, at:]),
        (down.at[rows:, rest:], packed.at[rest:, at:]),
    ]


def pack_kernel(gate, up, down, rest, packed):
    at = 0
    for piece in (gate, up, down, rest):
        packed[:, at : at + piece.shape[1]] = piece[...]
        at += piece.shape[1]


def unpack_kernel(packed, gate, up, down, sems):
    moves = [(source, target) for target, source in pack_moves(gate, up, down, packed)]
    for move in copies(moves, sems):
        move.wait()


def expert_kernel(
    rows, weights, out, pair, sums, rows_v, gate_up_v, down_v, pre_v, grad_v, hidden, pre, sums_v,
    out_v, pair_v, sems
):
    part, rest = down_v.shape[2], down_v.shape[1] - down_v.shape[2]
    hidden_width = down_v.shape[1]
    both = 2 * hidden_width
    last = both + part
    pairs = []
    for j in range(4):
        pairs += [
            (rows.at[:, j * part : (j + 1) * part], rows_v.at[j]),
            (weights.at[j, :, :both], gate_up_v.at[j]),
        ]
    for j in range(4):
        pairs += [
            (rows.at[:, (4 + j) * part : (5 + j) * part], rows_v.at[4 + j]),
            (weights.at[j, :, both:last], down_v.at[j, :part]),
            (weights.at[j, :rest, last:], down_v.at[j, part:, :rest]),
            (weights.at[j, rest:, last:], down_v.at[j, part:, rest:]),
        ]
    moves = copies(pairs, sems)
    for j in range(4):
        moves[2 * j].wait()
        moves[2 * j + 1].wait()
        product = dot(rows_v[j], gate_up_v[j], 1, 0)
        pre_v[...] = product if j == 0 else pre_v[...] + product
    for j in range(4):
        for move in moves[8 + 4 * j : 12 + 4 * j]:
            move.wait()
        product = dot(rows_v[4 + j], down_v[j], 1, 1)
        grad_v[...] = product if j == 0 else grad_v[...] + product
    step = 128
    for i in range(0, pre_v.shape[0], step):
        at = slice(i, i + step)
        gate_vals, up_vals = pre_v[at, :hidden_width], pre_v[at, hidden_width:]
        sig_vals = 1.0 / (1.0 + jnp.exp(-gate_vals))
        act_vals = gate_vals * sig_vals
        hidden[at] = (act_vals * up_vals).astype(BF)
        slope_vals = sig_vals * (1.0 + gate_vals * (1.0 - sig_vals))
        pre[at, :hidden_width] = (grad_v[at] * up_vals * slope_vals).astype(BF)
        pre[at, hidden_width:] = (grad_v[at] * act_vals).astype(BF)
    outs = []

    def leave(source, target):
        outs.append(pltpu.make_async_copy(source, target, sems.at[len(moves) + len(outs)]))
        outs[-1].start()

    for j in range(4):
        sums_v[j, :, :both] = dot(rows_v[j], pre[...], 0, 0).astype(BF)
        down_sum = dot(hidden[...], rows_v[4 + j], 0, 0).astype(BF)
        sums_v[j, :, both:last] = down_sum[:part]
        sums_v[j, :rest, last:] = down_sum[part:, :rest]
        sums_v[j, rest:, last:] = down_sum[part:, rest:]
        leave(sums_v.at[j], sums.at[j * part : (j + 1) * part])
    for j in range(4):
        at = slice(j * part, (j + 1) * part)
        pair_v[j] = dot(pre[...], gate_up_v[j], 1, 1).astype(BF)
        leave(pair_v.at[j], pair.at[:, at])
        out_v[j] = dot(hidden[...], down_v[j], 1, 0).astype(BF)
        leave(out_v.at[j], out.at[:, at])
    for move in outs:
        move.wait()


def combine_kernel(back, sources, weights, select, place, out, back_v, cot_v, sems):
    width = back.shape[1]
    moves = copies([(back, back_v), (sources.at[:, width : 2 * width], cot_v)], sems)
    high = weights[...].astype(BF)
    mid = (weights[...] - high.astype(F32)).astype(BF)
    moves[0].wait()
    out[:, :width] = dot(high, back_v[...], 1, 0) + dot(mid, back_v[...], 1, 0)
    moves[1].wait()
    products = dot(cot_v[...], back_v[...], 1, 1) * select[...].astype(F32)
    group = dot(products, place[...], 1, 0, lax.Precision.HIGHEST)
    high = group.astype(BF).astype(F32)
    lane = lax.broadcasted_iota(jnp.int32, group.shape, 1)
    out[:, width:] = jnp.where(lane < group.shape[1] // 2, high, group - high)


ANY = pl.BlockSpec(memory_space=pl.ANY)
VMEM = pl.BlockSpec(memory_space=pltpu.VMEM)


def call(kernel, in_specs, out_specs, outs, scratch, sems, limit):
    return pl.pallas_call(
        kernel,
        in_specs=in_specs,
        out_specs=out_specs,
        out_shape=[jax.ShapeDtypeStruct(*out) for out in outs],
        scratch_shapes=[*(pltpu.VMEM(*held) for held in scratch), pltpu.SemaphoreType.DMA((sems,))],
        compiler_params=pltpu.CompilerParams(vmem_limit_bytes=limit * 2**20),
        cost_estimate=pl.CostEstimate(flops=1, transcendentals=0, bytes_accessed=1),
    )


def pack(gate, up, down):
    rows, width = gate.shape
    step, rest = rows // 4, width - rows
    return pl.pallas_call(
        pack_kernel,
        grid=(4,),
        in_specs=[
            pl.BlockSpec((step, width), lambda i: (i, 0)),
            pl.BlockSpec((step, width), lambda i: (i, 0)),
            pl.BlockSpec((step, rows), lambda i: (i, 0)),
            pl.BlockSpec((step, rest), lambda i: (4 + i % 2, i // 2)),
        ],
        out_specs=pl.BlockSpec((step, 3 * width), lambda i: (i, 0)),
        out_shape=jax.ShapeDtypeStruct((rows, 3 * width), BF),
    )(gate, up, down, down)


def unpack(packed):
    rows, width = packed.shape[0], packed.shape[1] // 3
    outs = [((rows, width), BF), ((rows, width), BF), ((width, rows), BF)]
    return call(unpack_kernel, [VMEM], [ANY] * 3, outs, [], 5, 16)(packed)


def pieces(value):
    high = lax.reduce_precision(value, 8, 7)
    mid = lax.reduce_precision(value - high, 8, 7)
    return high, mid, value - high - mid


def body(tokens, expert_ids, gate_probs, grad_out, w_gate, w_up, w_down):
    me = lax.axis_index("expert")
    z, first = me % 16 // 2, me % 2 == 0
    rows, width = tokens.shape
    top = expert_ids.shape[1]
    hidden_width = w_gate.shape[2]
    part = width // 4
    count = 8
    held = count * rows

    experts = lax.all_gather(pack(w_gate[0], w_up[0], w_down[0]), "dp")

    meta = jnp.concatenate(
        [expert_ids.astype(F32), *pieces(gate_probs), jnp.zeros((rows, META - 4 * top), F32)],
        axis=1,
    ).astype(BF)
    gathered = gather_z(jnp.concatenate([tokens, grad_out, meta], axis=1), first)
    meta = gathered[:, 2 * width :].astype(F32)
    sources = gathered[:, : 2 * width]

    group = jnp.arange(8, dtype=jnp.int32)
    dest = (group // 2 * 16 + z * 2 + group % 2).astype(F32)[None, :]
    match = [meta[:, k : k + 1] == dest for k in range(top)]
    probs = meta[:, top : 2 * top] + meta[:, 2 * top : 3 * top] + meta[:, 3 * top : 4 * top]
    holds = sum(hit.astype(F32) for hit in match)
    weight = sum(jnp.where(hit, probs[:, k : k + 1], 0.0) for k, hit in enumerate(match))
    token_id = np.arange(held)
    slot_id = np.arange(8 * count * SLOTS)
    earlier = (token_id[None, :] < token_id[:, None]) & (
        token_id[None, :] // rows == token_id[:, None] // rows
    )
    spread = jnp.asarray(slot_id[None, :] // (count * SLOTS) == np.arange(8)[:, None], F32)
    rank = dot(jnp.asarray(earlier, BF), holds.astype(BF), 1, 0)
    rank = dot(jnp.where(holds > 0, rank, -1.0).astype(BF), spread.astype(BF), 1, 0)
    wanted = np.where(
        slot_id[None, :] // SLOTS % count == token_id[:, None] // rows, slot_id[None, :] % SLOTS, -2
    )
    fills = rank == jnp.asarray(wanted, F32)
    select = fills.astype(BF)
    weights = jnp.where(fills, dot(weight, spread, 1, 0, lax.Precision.HIGHEST), 0.0)
    slot_weight = dot(weights, jnp.ones((held, 1), F32), 0, 0, lax.Precision.HIGHEST)

    scale = jnp.where(jnp.arange(2 * width)[None, :] < width, 1.0, slot_weight)
    arrived = swap_rows((dot(select, sources, 0, 0) * scale).astype(BF))

    slots = arrived.shape[0]
    wide = (slots, 2 * hidden_width)
    expert_out, grad_pair, sums = call(
        expert_kernel,
        [ANY] * 2,
        [ANY, ANY, ANY],
        [((slots, width), BF), ((slots, width), BF), ((width, 3 * hidden_width), BF)],
        [
            ((8, slots, part), BF),
            ((4, part, 2 * hidden_width), BF),
            ((4, hidden_width, part), BF),
            (wide, F32),
            ((slots, hidden_width), F32),
            ((slots, hidden_width), BF),
            (wide, BF),
            ((4, part, 3 * hidden_width), BF),
            ((4, slots, part), BF),
            ((4, slots, part), BF),
        ],
        36,
        56,
    )(arrived, experts)
    weight_grads = lax.psum_scatter(sums, "dp", scatter_dimension=0, tiled=True)

    back_grads = swap_rows(grad_pair)
    expert_out, back_grads = lax.optimization_barrier((expert_out, back_grads))
    back_out = swap_rows(expert_out)
    lane = jnp.arange(META, dtype=jnp.int32)[None, :] % (META // 2)
    place = (lane == z * 8 + jnp.asarray(slot_id // (count * SLOTS), jnp.int32)[:, None]).astype(F32)
    (layer_part,) = call(
        combine_kernel,
        [ANY, ANY, VMEM, VMEM, VMEM],
        [VMEM],
        [((held, width + META), F32)],
        [((slots, width), BF), ((held, width), BF)],
        2,
        32,
    )(back_out, gathered, weights, select, place)
    layer_sum = scatter_z(layer_part, first)
    grad_tokens = scatter_z(dot(select, back_grads, 1, 0), first).astype(BF)
    layer_out = layer_sum[:, :width].astype(BF)
    prob_sum = layer_sum[:, width : width + META // 2] + layer_sum[:, width + META // 2 :]
    named = expert_ids % 16 // 2 * 8 + expert_ids // 16 * 2 + expert_ids % 2
    named = named[:, :, None] == jnp.arange(META // 2, dtype=jnp.int32)
    grad_probs = jnp.sum(jnp.where(named, prob_sum[:, None, :], 0.0), axis=2)
    grad_gate, grad_up, grad_down = unpack(weight_grads)
    return layer_out, grad_tokens, grad_probs, grad_gate[None], grad_up[None], grad_down[None]


def solution(mesh):
    return jax.shard_map(
        body,
        mesh=mesh,
        in_specs=(
            P(("dp", "expert"), None),
            P(("dp", "expert"), None),
            P(("dp", "expert"), None),
            P(("dp", "expert"), None),
            P("expert", "dp", None),
            P("expert", "dp", None),
            P("expert", None, "dp"),
        ),
        out_specs=(
            P(("dp", "expert"), None),
            P(("dp", "expert"), None),
            P(("dp", "expert"), None),
            P("expert", "dp", None),
            P("expert", "dp", None),
            P("expert", None, "dp"),
        ),
        check_vma=False,
    )
```
